128 devices in a mesh: leaf: 128 (over y, x, z, core).
Axes of the slice: x: 4, y: 4, z: 4, core: 2. Of those that a mesh axis runs over, the one named last changes fastest.
Arguments:
- leaf_bases: float32 [4096, 64, 256], P('leaf'), may hold values from -0.4 to 0.4
- transfers: float32 [8064, 64, 64], P('leaf')
- top_transfers: float32 [126, 64, 64], replicated
- couplings: float32 [7168, 8, 64, 64], P('leaf'), may hold values from -6 to 6
- coupling_cols: int32 [7168, 8], P('leaf'), may hold values from 0 to 7167, as said below
Outputs:
- new_leaf_bases: float32 [4096, 64, 256], P('leaf')
- new_transfers: float32 [8064, 64, 64], P('leaf')
- new_top: float32 [126, 64, 64], replicated
- root_factor: float32 [64, 64], replicated
- new_couplings: float32 [7168, 8, 64, 64], P('leaf')
The draws below stay inside these ranges and needn't reach their ends.
Inputs may be any that keep to these rules, and one draw needn't show every extreme that they name: `coupling_cols`: each entry names a cluster of the same tree level as its row's cluster, never that cluster itself, stored on a device at most 8 away from the row's device; the first two entries of every row lie exactly 8 devices away.
All inputs are finite; a program needn't handle non-finite values.
Results may differ from the reference program's by a relative error of at most 0.0001.
Values sent between devices are 32-bit elements; how exact they have to be, the bound alone decides.
No kernel may reach another device: no remote copies, remote signals or barrier semaphores. Data moves between devices by JAX's collectives and lax.ppermute only.
A program may use at most 256 MiB of HBM per device.

```python
import jax
import jax.numpy as jnp
from jax import lax

RANK = 64
POINTS = 256
LEAF_DEV = 32
CPL = 8
HOP = 8
LEAVES = 4096
TRANS_DEV = 63
TRANSFERS = 8064
ROW_DEV = 56
ROWS = 7168
TOP = 126
N_LEAF = 128


def transfer_draw(key, amount):
    diag_key, noise_key = jax.random.split(key)
    diagonal = jax.random.uniform(diag_key, (amount, RANK), jnp.float32, 0.6, 1.4)
    noise = jax.random.normal(noise_key, (amount, RANK, RANK), jnp.float32) * (0.5 / RANK ** 0.5)
    identity = jnp.eye(RANK, dtype=jnp.float32)
    return (diagonal[:, :, None] * identity + noise) * 0.7071


def draw_transfers(key, part):
    return transfer_draw(jax.random.fold_in(key, 11), TRANSFERS)


def draw_top_transfers(key, part):
    return transfer_draw(jax.random.fold_in(key, 23), TOP)


def draw_coupling_cols(key, part):
    shift_key, index_key = jax.random.split(jax.random.fold_in(key, 37))
    row_ids = jnp.arange(ROWS, dtype=jnp.int32)
    device_of = row_ids // ROW_DEV
    local = row_ids % ROW_DEV
    mid_start = LEAF_DEV
    top_start = LEAF_DEV + LEAF_DEV // 2
    base = jnp.where(local < mid_start, 0, jnp.where(local < top_start, mid_start, top_start))
    amount = jnp.where(local < mid_start, LEAF_DEV, jnp.where(local < top_start, LEAF_DEV // 2, LEAF_DEV // 4))
    offsets = jax.random.randint(shift_key, (ROWS, CPL), -HOP, HOP + 1)
    down_first = jnp.where(device_of >= HOP, -HOP, HOP)
    up_first = jnp.where(device_of + HOP <= N_LEAF - 1, HOP, -HOP)
    offsets = offsets.at[:, 0].set(down_first)
    offsets = offsets.at[:, 1].set(up_first)
    target = jnp.clip(device_of[:, None] + offsets, 0, N_LEAF - 1)
    picked = jax.random.randint(index_key, (ROWS, CPL), 0, 64 * LEAF_DEV) % amount[:, None]
    picked = picked.at[:, 0].set(jnp.where(local == base, 0, picked[:, 0]))
    picked = picked.at[:, 1].set(jnp.where(local == base + amount - 1, amount - 1, picked[:, 1]))
    itself = (target == device_of[:, None]) & (base[:, None] + picked == local[:, None])
    moved = jnp.where(device_of < N_LEAF - 1, device_of + 1, device_of - 1)
    target = jnp.where(itself, moved[:, None], target)
    return (target * ROW_DEV + base[:, None] + picked).astype(jnp.int32)


def block_scale(rng, dims, cuts, least, high):
    def one(axis_at, blocks):
        heights = jax.random.uniform(jax.random.fold_in(jax.random.fold_in(rng, 6), axis_at), (blocks,), jnp.float32, least / len(cuts), high / len(cuts))
        return jnp.repeat(jnp.exp(heights), dims[axis_at] // blocks).reshape((-1,) + (1,) * (len(dims) - axis_at - 1))

    level = one(*cuts[0])
    for cut in cuts[1:]:
        level = level * one(*cut)
    return level


def scatter_about(own_key, dims, spread, reach, cuts=(), kind=jnp.bfloat16):
    values = jax.random.normal(own_key, dims, jnp.float32) * spread
    if len(cuts) > 0:
        values = block_scale(own_key, dims, cuts, -0.22, 0.18) * values
    return jnp.clip(values, min=-reach, max=reach).astype(kind)


def setup_inputs(seed: int = 0) -> dict:
    arg_keys = jax.random.split(jax.random.key(seed), 6)
    leaf_bases = scatter_about(arg_keys[0], (LEAVES, RANK, POINTS), 0.0625, 0.4, ((0, 128),), jnp.float32)
    transfers = draw_transfers(jax.random.fold_in(arg_keys[5], 71), 0)
    top_transfers = draw_top_transfers(jax.random.fold_in(arg_keys[5], 71), 0)
    couplings = scatter_about(arg_keys[3], (ROWS, CPL, RANK, RANK), 1.0, 6.0, ((0, 128),), jnp.float32)
    coupling_cols = draw_coupling_cols(jax.random.fold_in(arg_keys[5], 71), 0)
    return dict(leaf_bases=leaf_bases, transfers=transfers, top_transfers=top_transfers, couplings=couplings, coupling_cols=coupling_cols)


PRECISE = lax.Precision.HIGHEST

def inverse_lower(factor):
    identity = jnp.broadcast_to(jnp.eye(factor.shape[-1], dtype=factor.dtype), factor.shape)
    return lax.linalg.triangular_solve(factor, identity, left_side=True, lower=True)

def join_pairs(lower_part, upper_part):
    gram_matrix = jnp.einsum('bki,bkj->bij', lower_part, lower_part, precision=PRECISE)
    gram_matrix = gram_matrix + jnp.einsum('bki,bkj->bij', upper_part, upper_part, precision=PRECISE)
    factor = jnp.linalg.cholesky(gram_matrix)
    inverse = inverse_lower(factor)
    stacked = jnp.concatenate([lower_part, upper_part], axis=1)
    solved = jnp.einsum('bki,bji->bkj', stacked, inverse, precision=PRECISE)
    rank_size = lower_part.shape[1]
    return (factor, solved[:, 0:rank_size], solved[:, rank_size:])

def carry_up(factor, transfer):
    return jnp.einsum('bki,bkj->bij', factor, transfer, precision=PRECISE)

def pair_order(lower_q, upper_q):
    return jnp.stack([lower_q, upper_q], axis=1).reshape((-1,) + lower_q.shape[1:])

def reference(leaf_bases, transfers, top_transfers, couplings, coupling_cols):
    tree_depth = LEAF_DEV.bit_length() - 1
    top_depth = N_LEAF.bit_length() - 1
    blocks = transfers.reshape(N_LEAF, TRANS_DEV, RANK, RANK)

    def local_level(height):
        offset = 2 * LEAF_DEV - 2 * (LEAF_DEV >> height)
        return blocks[:, offset:offset + (LEAF_DEV >> height)].reshape(-1, RANK, RANK)
    gram_matrix = jnp.einsum('bip,bjp->bij', leaf_bases, leaf_bases, precision=PRECISE)
    factor = jnp.linalg.cholesky(gram_matrix)
    new_leaves = jnp.einsum('bij,bjp->bip', inverse_lower(factor), leaf_bases, precision=PRECISE)
    factors = [factor]
    new_levels = []
    carried = carry_up(factor, local_level(0))
    for height in range(1, tree_depth + top_depth + 1):
        factor, lower_q, upper_q = join_pairs(carried[0::2], carried[1::2])
        new_levels.append(pair_order(lower_q, upper_q))
        factors.append(factor)
        if height <= tree_depth:
            carried = carry_up(factor, local_level(height))
        elif height < tree_depth + top_depth:
            node_level = tree_depth + top_depth - height
            first_node = 2 ** node_level - 2
            carried = carry_up(factor, top_transfers[first_node:first_node + 2 ** node_level])
    root_factor = factors[-1][0].T
    new_transfers = jnp.concatenate([new_levels[height].reshape(N_LEAF, -1, RANK, RANK) for height in range(tree_depth + 1)], axis=1).reshape(-1, RANK, RANK)
    new_top = jnp.concatenate(new_levels[tree_depth + 1:tree_depth + top_depth][::-1], axis=0)
    packed = jnp.concatenate([factors[height].reshape(N_LEAF, -1, RANK, RANK) for height in range(3)], axis=1).reshape(-1, RANK, RANK)

    def one_device(device_index):
        row_start = device_index * ROW_DEV
        row_factor = lax.dynamic_slice_in_dim(packed, row_start, ROW_DEV, 0)
        block = lax.dynamic_slice_in_dim(couplings, row_start, ROW_DEV, 0)
        columns = lax.dynamic_slice_in_dim(coupling_cols, row_start, ROW_DEV, 0)
        column_factor = jnp.take(packed, columns.reshape(-1), axis=0).reshape(ROW_DEV, CPL, RANK, RANK)
        left_side = jnp.einsum('rki,rckl->rcil', row_factor, block, precision=PRECISE)
        return jnp.einsum('rcil,rclj->rcij', left_side, column_factor, precision=PRECISE)
    new_couplings = lax.map(one_device, jnp.arange(N_LEAF, dtype=jnp.int32)).reshape(ROWS, CPL, RANK, RANK)
    return (new_leaves, new_transfers, new_top, root_factor, new_couplings)
```

```python
import functools

import jax
import jax.numpy as jnp
from jax import lax
from jax.experimental import pallas as pl
from jax.experimental.pallas import tpu as pltpu
from jax.sharding import PartitionSpec as P

RANK = 64
LEAF = 32
NODES = 63
ROW = 56
CPL = 8
QUART = 14
UNIT = QUART + 1
COLUMN = 8
TOPN = 127
VMEM_LIMIT = 48 * 1024 * 1024
F32 = jnp.float32
BF16 = jnp.bfloat16
FULL = lax.Precision.HIGHEST

NN = (((1,), (0,)), ((), ()))
NT = (((1,), (1,)), ((), ()))
TN = (((0,), (0,)), ((), ()))


def exact(a, b, dims):
    return lax.dot_general(a, b, dims, precision=FULL, preferred_element_type=F32)


def split(a):
    high = a.astype(BF16)
    return high, (a - high.astype(F32)).astype(BF16)


def three(a, b, dims):
    ah, al = a
    bh, bl = b
    dot = functools.partial(lax.dot_general, dimension_numbers=dims, preferred_element_type=F32)
    return dot(ah, bh) + (dot(ah, bl) + dot(al, bh))


def mul3(a, b, dims):
    return three(split(a), split(b), dims)


def params():
    return pltpu.CompilerParams(vmem_limit_bytes=VMEM_LIMIT)


def load_lanes(g_ref, w_ref):
    place = lax.broadcasted_iota(jnp.int32, (RANK, 128), 0)

    def body(i, carry):
        block = g_ref[pl.ds(i, 128, stride=RANK), :].T
        w_ref[i, 0:RANK, :] = block[0:RANK]
        w_ref[i, RANK:128, :] = jnp.where(place == i, 1.0, 0.0).astype(F32)
        return carry

    lax.fori_loop(0, RANK, body, 0, unroll=4)


def eliminate(w_ref):
    for band in range(16):
        q = band // 2
        lo, hi = 8 * q, RANK + 8 * (q + 1)
        first = 4 * band
        rows = tuple(w_ref[first + a, lo:hi, :] for a in range(4))

        def step(k, rows):
            src = w_ref[k, lo:hi, :]
            return tuple(
                rows[a] - w_ref[k, first + a : first + a + 1, :] * src for a in range(4)
            )

        if first > 0:
            rows = lax.fori_loop(0, first, step, rows, unroll=2)
        rows = list(rows)
        for a in range(4):
            at = first + a - lo
            for b in range(a):
                rows[a] = rows[a] - rows[b][at : at + 1] * rows[b]
            pivot = rows[a][at : at + 1]
            scale = lax.rsqrt(pivot)
            scale = scale * (1.5 - 0.5 * pivot * scale * scale)
            rows[a] = rows[a] * scale
            w_ref[first + a, lo:hi, :] = rows[a]


def clear_lower(w_ref):
    place = lax.broadcasted_iota(jnp.int32, (RANK, 128), 0)

    def body(i, carry):
        w_ref[i, 0:RANK, :] = jnp.where(place >= i, w_ref[i, 0:RANK, :], 0.0)
        return carry

    lax.fori_loop(0, RANK, body, 0, unroll=4)


def store_lanes(w_ref, um_ref, amount):
    def body(i, carry):
        block = w_ref[i].T
        um_ref[pl.ds(i, amount, stride=RANK), :] = block[0:amount]
        return carry

    lax.fori_loop(0, RANK, body, 0, unroll=4)


def gram_kernel(v_ref, e_ref, g_ref, c_ref):
    def leaf(b, carry):
        v = v_ref[b]
        g_ref[pl.ds(b * RANK, RANK), 0:RANK] = exact(v, v, NT)
        return carry

    lax.fori_loop(0, LEAF, leaf, 0, unroll=4)

    def parent(p, carry):
        a = 2 * (p - LEAF)
        ea, eb = e_ref[a], e_ref[a + 1]
        ga = g_ref[pl.ds(a * RANK, RANK), 0:RANK]
        gb = g_ref[pl.ds((a + 1) * RANK, RANK), 0:RANK]
        both = jnp.concatenate([exact(ga, ea, NN), exact(gb, eb, NN)], axis=0)
        g_ref[pl.ds(p * RANK, RANK), 0:RANK] = exact(
            jnp.concatenate([ea, eb], axis=0), both, TN
        )
        return carry

    start, amount = LEAF, LEAF // 2
    while amount >= 1:
        lax.fori_loop(start, start + amount, parent, 0, unroll=min(amount, 4))
        start, amount = start + amount, amount // 2
    root = e_ref[NODES - 1]
    top = exact(root, exact(g_ref[(NODES - 1) * RANK : NODES * RANK, 0:RANK], root, NN), TN)
    c_ref[:, 0:RANK] = top[0:32]
    c_ref[:, RANK:128] = top[32:64]
    g_ref[NODES * RANK :, :] = jnp.zeros_like(g_ref[NODES * RANK :, :])


def gram_call(v, e):
    return pl.pallas_call(
        gram_kernel,
        out_shape=(
            jax.ShapeDtypeStruct((128 * RANK, 128), F32),
            jax.ShapeDtypeStruct((32, 128), F32),
        ),
        compiler_params=params(),
        cost_estimate=pl.CostEstimate(flops=400_000_000, bytes_accessed=8_000_000, transcendentals=0),
        name="gram_up",
    )(v, e)


def factor_kernel(g_ref, um_ref, unit_ref, w_ref):
    load_lanes(g_ref, w_ref)
    eliminate(w_ref)
    clear_lower(w_ref)
    place = lax.broadcasted_iota(jnp.int32, (RANK, 128), 0)
    rows = w_ref.reshape(RANK * 128, 128)

    def pack(i, diag):
        upper = w_ref[i, 0:RANK, :]
        lower = rows[pl.ds(i, RANK, stride=128), :]
        other = pltpu.roll(lower, 128 - 2 * QUART, axis=1)
        mixed = jnp.where(place >= i, upper, other)
        both = jnp.concatenate([mixed, pltpu.roll(mixed, 128 - QUART, axis=1)], axis=0).T
        unit_ref[pl.ds(i, QUART, stride=RANK), :] = both[0:QUART]
        return jnp.where(place == i, lower, diag)

    diag = lax.fori_loop(0, RANK, pack, jnp.zeros((RANK, 128), F32), unroll=4)
    unit_ref[QUART * RANK :, :] = jnp.concatenate([diag, diag], axis=0).T[0:RANK]
    store_lanes(w_ref, um_ref, RANK)


def factor_call(g):
    return pl.pallas_call(
        factor_kernel,
        out_shape=(
            jax.ShapeDtypeStruct((RANK * RANK, 128), F32),
            jax.ShapeDtypeStruct((UNIT * RANK, 128), F32),
        ),
        scratch_shapes=[pltpu.VMEM((RANK, 128, 128), F32)],
        compiler_params=params(),
        cost_estimate=pl.CostEstimate(flops=400_000_000, bytes_accessed=8_000_000, transcendentals=0),
        name="factor_local",
    )(g)


def apply_kernel(um_ref, v_ref, e_ref, leaves_ref, moved_ref):
    def leaf(b, carry):
        m = um_ref[b, :, RANK:128]
        leaves_ref[b] = mul3(m, v_ref[b], NN)
        return carry

    lax.fori_loop(0, LEAF, leaf, 0, unroll=2)

    def parent(p, carry):
        a = 2 * (p - LEAF)
        pa = mul3(um_ref[a, :, 0:RANK], e_ref[a], NN)
        pb = mul3(um_ref[a + 1, :, 0:RANK], e_ref[a + 1], NN)
        q = mul3(jnp.concatenate([pa, pb], axis=0), um_ref[p, :, RANK:128], NT)
        moved_ref[a] = q[0:RANK]
        moved_ref[a + 1] = q[RANK:128]
        return carry

    lax.fori_loop(LEAF, NODES, parent, 0, unroll=2)
    moved_ref[NODES - 1] = mul3(um_ref[NODES - 1, :, 0:RANK], e_ref[NODES - 1], NN)


def apply_call(um, v, e):
    return pl.pallas_call(
        apply_kernel,
        out_shape=(
            jax.ShapeDtypeStruct(v.shape, F32),
            jax.ShapeDtypeStruct(e.shape, F32),
        ),
        compiler_params=params(),
        cost_estimate=pl.CostEstimate(flops=600_000_000, bytes_accessed=20_000_000, transcendentals=0),
        name="apply_local",
    )(um, v, e)


def top_kernel(own_ref, c_ref, e_ref, p_ref, new_ref, root_ref, mine_ref, g_ref, w_ref, um_ref):
    def wide(d):
        x = c_ref[d]
        return jnp.concatenate([x[:, 0:RANK], x[:, RANK:128]], axis=0)

    def first(p, carry):
        g_ref[pl.ds((63 + p) * RANK, RANK), 0:RANK] = wide(2 * p) + wide(2 * p + 1)
        return carry

    lax.fori_loop(0, 64, first, 0, unroll=4)

    def join(n, carry):
        c = 2 * n + 1
        ea, eb = e_ref[c - 1], e_ref[c]
        ga = g_ref[pl.ds(c * RANK, RANK), 0:RANK]
        gb = g_ref[pl.ds((c + 1) * RANK, RANK), 0:RANK]
        both = jnp.concatenate([exact(ga, ea, NN), exact(gb, eb, NN)], axis=0)
        g_ref[pl.ds(n * RANK, RANK), 0:RANK] = exact(
            jnp.concatenate([ea, eb], axis=0), both, TN
        )
        return carry

    for level in range(5, -1, -1):
        begin = 2**level - 1
        lax.fori_loop(begin, 2 * begin + 1, join, 0, unroll=min(2**level, 4))
    g_ref[TOPN * RANK :, :] = jnp.zeros_like(g_ref[TOPN * RANK :, :])
    load_lanes(g_ref, w_ref)
    eliminate(w_ref)
    clear_lower(w_ref)
    store_lanes(w_ref, um_ref, 128)

    def out(n, carry):
        c = 2 * n + 1
        pa = mul3(um_ref[pl.ds(c * RANK, RANK), 0:RANK], e_ref[c - 1], NN)
        pb = mul3(um_ref[pl.ds((c + 1) * RANK, RANK), 0:RANK], e_ref[c], NN)
        m = um_ref[pl.ds(n * RANK, RANK), RANK:128]
        q = mul3(jnp.concatenate([pa, pb], axis=0), m, NT)
        new_ref[c - 1] = q[0:RANK]
        new_ref[c] = q[RANK:128]
        return carry

    lax.fori_loop(0, 63, out, 0, unroll=3)
    root_ref[...] = um_ref[0:RANK, 0:RANK]
    up = 63 + own_ref[0] // 2
    mine_ref[...] = mul3(p_ref[...], um_ref[pl.ds(pl.multiple_of(up * RANK, RANK), RANK), RANK:128], NT)


def top_call(own, c, e, p):
    vm = pl.BlockSpec(memory_space=pltpu.VMEM)
    return pl.pallas_call(
        top_kernel,
        in_specs=[pl.BlockSpec(memory_space=pltpu.SMEM), vm, vm, vm],
        out_shape=(
            jax.ShapeDtypeStruct(e.shape, F32),
            jax.ShapeDtypeStruct((RANK, RANK), F32),
            jax.ShapeDtypeStruct((RANK, RANK), F32),
        ),
        scratch_shapes=[
            pltpu.VMEM((128 * RANK, 128), F32),
            pltpu.VMEM((RANK, 128, 128), F32),
            pltpu.VMEM((128 * RANK, 128), F32),
        ],
        compiler_params=params(),
        cost_estimate=pl.CostEstimate(flops=1_000_000_000, bytes_accessed=60_000_000, transcendentals=0),
        name="top_tree",
    )(own, c, e, p)


def couple_kernel(where_ref, s_ref, um_ref, win_ref, out_ref):
    row = pl.program_id(0)
    down = lax.broadcasted_iota(jnp.int32, (RANK, RANK), 0)
    over = lax.broadcasted_iota(jnp.int32, (RANK, RANK), 1)
    parts = []
    for c in range(CPL):
        code = where_ref[row, c]
        unit = code // 64
        local = code % 64
        quarter = local // QUART
        x = win_ref[unit * UNIT + local % QUART]
        half = quarter % 2
        plain = jnp.where(half == 0, x[:, 0:RANK], x[:, RANK:128])
        t = x.T
        turned = jnp.where(half == 0, t[0:RANK], t[RANK:128])
        diag = win_ref[unit * UNIT + QUART, pl.ds(local, 1), 0:RANK]
        second = quarter >= 2
        strict = jnp.where(second, plain, turned)
        on = jnp.where(second, jnp.broadcast_to(diag, (RANK, RANK)), turned)
        lower = jnp.where(down > over, strict, jnp.where(down == over, on, 0.0))
        parts.append(mul3(s_ref[0, c], lower, NN))
    u = split(um_ref[row, :, 0:RANK])
    for c in range(CPL):
        out_ref[0, c] = three(u, split(parts[c]), NN)


def couple_call(where, s, um, win):
    return pl.pallas_call(
        couple_kernel,
        grid_spec=pltpu.PrefetchScalarGridSpec(
            num_scalar_prefetch=1,
            grid=(ROW,),
            in_specs=[
                pl.BlockSpec((1, CPL, RANK, RANK), lambda r, w: (r, 0, 0, 0)),
                pl.BlockSpec(memory_space=pltpu.VMEM),
                pl.BlockSpec(memory_space=pltpu.VMEM),
            ],
            out_specs=pl.BlockSpec((1, CPL, RANK, RANK), lambda r, w: (r, 0, 0, 0)),
        ),
        out_shape=jax.ShapeDtypeStruct(s.shape, F32),
        compiler_params=params(),
        cost_estimate=pl.CostEstimate(flops=1_500_000_000, bytes_accessed=45_000_000, transcendentals=0),
        name="couple",
    )(where, s, um, win)


def shifted(array, axis, by):
    devices = lax.axis_size(axis)
    pairs = [(i, i + by) for i in range(devices) if 0 <= i + by < devices]
    return lax.ppermute(array, axis, pairs)


def on_device(leaf_bases, transfers, top_transfers, couplings, coupling_cols):
    devices = lax.axis_size("leaf")
    own = lax.axis_index("leaf").astype(jnp.int32)
    grams, carried = gram_call(leaf_bases, transfers)
    frontier = lax.all_gather(carried, "leaf", axis=0, tiled=False)
    um, unit = factor_call(grams)
    um = um.reshape(RANK, RANK, 128)
    unit = unit.reshape(UNIT, RANK, 128)
    trio = jnp.concatenate([shifted(unit, "leaf", COLUMN), unit, shifted(unit, "leaf", -COLUMN)], axis=0)
    groups = [[c * COLUMN + j for j in range(COLUMN)] for c in range(devices // COLUMN)]
    window = lax.all_gather(trio, "leaf", axis_index_groups=groups, axis=0, tiled=True)
    device_of = coupling_cols // ROW
    side = device_of // COLUMN - own // COLUMN + 1
    where = (device_of % COLUMN * 3 + side) * 64 + coupling_cols % ROW
    new_leaves, moved = apply_call(um, leaf_bases, transfers)
    new_top, root_factor, mine = top_call(
        own.reshape(1), frontier, top_transfers, moved[NODES - 1]
    )
    new_transfers = moved.at[NODES - 1].set(mine)
    new_couplings = couple_call(where, couplings, um, window)
    return (new_leaves, new_transfers, new_top, root_factor, new_couplings)


def solution(mesh):
    in_specs = (
        P("leaf", None, None),
        P("leaf", None, None),
        P(),
        P("leaf", None, None, None),
        P("leaf", None),
    )
    out_specs = (
        P("leaf", None, None),
        P("leaf", None, None),
        P(),
        P(),
        P("leaf", None, None, None),
    )
    return jax.shard_map(
        on_device, mesh=mesh, in_specs=in_specs, out_specs=out_specs, check_vma=False
    )
```

```python
import functools

import jax
import jax.numpy as jnp
from jax import lax
from jax.experimental import pallas as pl
from jax.experimental.pallas import tpu as pltpu
from jax.sharding import PartitionSpec as P

RANK = 64
LEAF = 32
NODES = 63
ROW = 56
CPL = 8
QUART = 14
UNIT = QUART + 1
COLUMN = 8
TOPN = 127
ROWS_STEP = 8
VMEM_LIMIT = 48 * 1024 * 1024
F32 = jnp.float32
BF16 = jnp.bfloat16
FULL = lax.Precision.HIGHEST

NN = (((1,), (0,)), ((), ()))
NT = (((1,), (1,)), ((), ()))
TN = (((0,), (0,)), ((), ()))


def exact(a, b, dims):
    return lax.dot_general(a, b, dims, precision=FULL, preferred_element_type=F32)


def split(a):
    high = a.astype(BF16)
    return high, (a - high.astype(F32)).astype(BF16)


def three(a, b, dims):
    ah, al = a
    bh, bl = b
    dot = functools.partial(lax.dot_general, dimension_numbers=dims, preferred_element_type=F32)
    return dot(ah, bh) + (dot(ah, bl) + dot(al, bh))


def mul3(a, b, dims):
    return three(split(a), split(b), dims)


def cost(us):
    return pl.CostEstimate(flops=us * 1_000_000, bytes_accessed=us * 2_500_000, transcendentals=0)


def params():
    return pltpu.CompilerParams(vmem_limit_bytes=VMEM_LIMIT)


def load_lanes(g_ref, w_ref):
    place = lax.broadcasted_iota(jnp.int32, (RANK, 128), 0)

    def body(i, carry):
        block = g_ref[pl.ds(i, 128, stride=RANK), :].T
        w_ref[i, 0:RANK, :] = block[0:RANK]
        w_ref[i, RANK:128, :] = jnp.where(place == i, 1.0, 0.0).astype(F32)
        return carry

    lax.fori_loop(0, RANK, body, 0, unroll=8)


def eliminate(w_ref):
    for band in range(16):
        q = band // 2
        lo, hi = 8 * q, RANK + 8 * (q + 1)
        first = 4 * band
        rows = tuple(w_ref[first + a, lo:hi, :] for a in range(4))

        def step(k, rows):
            src = w_ref[k, lo:hi, :]
            return tuple(
                rows[a] - w_ref[k, first + a : first + a + 1, :] * src for a in range(4)
            )

        if first > 0:
            rows = lax.fori_loop(0, first, step, rows, unroll=4)
        rows = list(rows)
        for a in range(4):
            at = first + a - lo
            for b in range(a):
                rows[a] = rows[a] - rows[b][at : at + 1] * rows[b]
            pivot = rows[a][at : at + 1]
            scale = lax.rsqrt(pivot)
            scale = scale * (1.5 - 0.5 * pivot * scale * scale)
            rows[a] = rows[a] * scale
            w_ref[first + a, lo:hi, :] = rows[a]


def store_lanes(w_ref, um_ref, amount):
    place = lax.broadcasted_iota(jnp.int32, (RANK, 128), 0)

    def body(i, carry):
        upper = jnp.where(place >= i, w_ref[i, 0:RANK, :], 0.0)
        block = jnp.concatenate([upper, w_ref[i, RANK:128, :]], axis=0).T
        um_ref[pl.ds(i, amount, stride=RANK), :] = block[0:amount]
        return carry

    lax.fori_loop(0, RANK, body, 0, unroll=8)


def block_at(n):
    return pl.ds(pl.multiple_of(n * RANK, RANK), RANK)


def gram_kernel(v_ref, e_ref, g_ref, c_ref):
    def leaf(b, carry):
        v = v_ref[b]
        g_ref[block_at(b), 0:RANK] = exact(v, v, NT)
        return carry

    lax.fori_loop(0, LEAF, leaf, 0, unroll=8)

    def parent(p, carry):
        a = 2 * (p - LEAF)
        ea, eb = e_ref[a], e_ref[a + 1]
        ga = g_ref[block_at(a), 0:RANK]
        gb = g_ref[block_at(a + 1), 0:RANK]
        both = jnp.concatenate([exact(ga, ea, NN), exact(gb, eb, NN)], axis=0)
        g_ref[block_at(p), 0:RANK] = exact(
            jnp.concatenate([ea, eb], axis=0), both, TN
        )
        return carry

    start, amount = LEAF, LEAF // 2
    while amount >= 1:
        lax.fori_loop(start, start + amount, parent, 0, unroll=min(amount, 16))
        start, amount = start + amount, amount // 2
    root = e_ref[NODES - 1]
    top = exact(root, exact(g_ref[(NODES - 1) * RANK : NODES * RANK, 0:RANK], root, NN), TN)
    c_ref[:, 0:RANK] = top[0:32]
    c_ref[:, RANK:128] = top[32:64]
    g_ref[NODES * RANK :, :] = jnp.zeros_like(g_ref[NODES * RANK :, :])


def gram_call(v, e):
    return pl.pallas_call(
        gram_kernel,
        out_shape=(
            jax.ShapeDtypeStruct((128 * RANK, 128), F32),
            jax.ShapeDtypeStruct((32, 128), F32),
        ),
        compiler_params=params(),
        cost_estimate=cost(12),
        name="gram_up",
    )(v, e)


def factor_kernel(g_ref, w_ref, unit_ref):
    load_lanes(g_ref, w_ref)
    eliminate(w_ref)
    place = lax.broadcasted_iota(jnp.int32, (RANK, 128), 0)
    rows = w_ref.reshape(RANK * 128, 128)

    def pack(i, diag):
        upper = w_ref[i, 0:RANK, :]
        lower = rows[pl.ds(i, RANK, stride=128), :]
        other = pltpu.roll(lower, 128 - 2 * QUART, axis=1)
        mixed = jnp.where(place >= i, upper, other)
        both = jnp.concatenate([mixed, pltpu.roll(mixed, 128 - QUART, axis=1)], axis=0).T
        unit_ref[pl.ds(i, QUART, stride=RANK), :] = both[0:QUART]
        return jnp.where(place == i, lower, diag)

    diag = lax.fori_loop(0, RANK, pack, jnp.zeros((RANK, 128), F32), unroll=8)
    unit_ref[QUART * RANK :, :] = jnp.concatenate([diag, diag], axis=0).T[0:RANK]


def factor_call(g):
    return pl.pallas_call(
        factor_kernel,
        out_shape=(
            jax.ShapeDtypeStruct((RANK, 128, 128), F32),
            jax.ShapeDtypeStruct((UNIT * RANK, 128), F32),
        ),
        compiler_params=params(),
        cost_estimate=cost(15),
        name="factor_local",
    )(g)


def turn_kernel(w_ref, um_ref):
    store_lanes(w_ref, um_ref, RANK)


def turn_call(w):
    return pl.pallas_call(
        turn_kernel,
        out_shape=jax.ShapeDtypeStruct((RANK * RANK, 128), F32),
        compiler_params=params(),
        cost_estimate=cost(6),
        name="turn_local",
    )(w)


def apply_kernel(um_ref, v_ref, e_ref, leaves_ref, moved_ref):
    def leaf(b, carry):
        m = um_ref[b, :, RANK:128]
        leaves_ref[b] = mul3(m, v_ref[b], NN)
        return carry

    lax.fori_loop(0, LEAF, leaf, 0, unroll=8)

    def parent(p, carry):
        a = 2 * (p - LEAF)
        pa = mul3(um_ref[a, :, 0:RANK], e_ref[a], NN)
        pb = mul3(um_ref[a + 1, :, 0:RANK], e_ref[a + 1], NN)
        q = mul3(jnp.concatenate([pa, pb], axis=0), um_ref[p, :, RANK:128], NT)
        moved_ref[a] = q[0:RANK]
        moved_ref[a + 1] = q[RANK:128]
        return carry

    lax.fori_loop(LEAF, NODES - 1, parent, 0, unroll=10)
    parent(NODES - 1, 0)
    moved_ref[NODES - 1] = mul3(um_ref[NODES - 1, :, 0:RANK], e_ref[NODES - 1], NN)


def apply_call(um, v, e):
    return pl.pallas_call(
        apply_kernel,
        out_shape=(
            jax.ShapeDtypeStruct(v.shape, F32),
            jax.ShapeDtypeStruct(e.shape, F32),
        ),
        compiler_params=params(),
        cost_estimate=cost(9),
        name="apply_local",
    )(um, v, e)


def top_gram_kernel(c_ref, e_ref, w_ref, g_ref):
    def wide(d):
        x = c_ref[d]
        return jnp.concatenate([x[:, 0:RANK], x[:, RANK:128]], axis=0)

    def first(p, carry):
        g_ref[block_at(63 + p), 0:RANK] = wide(2 * p) + wide(2 * p + 1)
        return carry

    lax.fori_loop(0, 64, first, 0, unroll=16)

    def join(n, carry):
        c = 2 * n + 1
        ea, eb = e_ref[c - 1], e_ref[c]
        ga = g_ref[block_at(c), 0:RANK]
        gb = g_ref[block_at(c + 1), 0:RANK]
        both = jnp.concatenate([exact(ga, ea, NN), exact(gb, eb, NN)], axis=0)
        g_ref[block_at(n), 0:RANK] = exact(jnp.concatenate([ea, eb], axis=0), both, TN)
        return carry

    for level in range(5, -1, -1):
        begin = 2**level - 1
        lax.fori_loop(begin, 2 * begin + 1, join, 0, unroll=min(2**level, 16))
    g_ref[TOPN * RANK :, :] = jnp.zeros_like(g_ref[TOPN * RANK :, :])
    load_lanes(g_ref, w_ref)
    eliminate(w_ref)


def top_gram_call(c, e):
    return pl.pallas_call(
        top_gram_kernel,
        out_shape=jax.ShapeDtypeStruct((RANK, 128, 128), F32),
        scratch_shapes=[pltpu.VMEM((128 * RANK, 128), F32)],
        compiler_params=params(),
        cost_estimate=cost(25),
        name="top_gram",
    )(c, e)


def top_out_kernel(own_ref, w_ref, e_ref, p_ref, new_ref, root_ref, mine_ref, um_ref):
    store_lanes(w_ref, um_ref, 128)

    def out(n, carry):
        c = 2 * n + 1
        pa = mul3(um_ref[block_at(c), 0:RANK], e_ref[c - 1], NN)
        pb = mul3(um_ref[block_at(c + 1), 0:RANK], e_ref[c], NN)
        m = um_ref[block_at(n), RANK:128]
        q = mul3(jnp.concatenate([pa, pb], axis=0), m, NT)
        new_ref[c - 1] = q[0:RANK]
        new_ref[c] = q[RANK:128]
        return carry

    lax.fori_loop(0, 63, out, 0, unroll=9)
    root_ref[...] = um_ref[0:RANK, 0:RANK]
    up = 63 + own_ref[0] // 2
    mine_ref[...] = mul3(p_ref[...], um_ref[block_at(up), RANK:128], NT)


def top_out_call(own, w, e, p):
    vm = pl.BlockSpec(memory_space=pltpu.VMEM)
    return pl.pallas_call(
        top_out_kernel,
        in_specs=[pl.BlockSpec(memory_space=pltpu.SMEM), vm, vm, vm],
        out_shape=(
            jax.ShapeDtypeStruct(e.shape, F32),
            jax.ShapeDtypeStruct((RANK, RANK), F32),
            jax.ShapeDtypeStruct((RANK, RANK), F32),
        ),
        scratch_shapes=[pltpu.VMEM((128 * RANK, 128), F32)],
        compiler_params=params(),
        cost_estimate=cost(17),
        name="top_out",
    )(own, w, e, p)


def left_kernel(s_ref, um_ref, z_ref):
    first = pl.program_id(0) * ROWS_STEP

    def one(r, carry):
        u = split(um_ref[first + r, :, 0:RANK])
        for c in range(CPL):
            z = three(u, split(s_ref[r, c]), NN)
            high = z.astype(BF16).astype(F32)
            z_ref[r, c] = jnp.concatenate([high, z - high], axis=1).astype(BF16)
        return carry

    lax.fori_loop(0, ROWS_STEP, one, 0, unroll=4)


def left_call(s, um):
    return pl.pallas_call(
        left_kernel,
        grid=(ROW // ROWS_STEP,),
        in_specs=[
            pl.BlockSpec((ROWS_STEP, CPL, RANK, RANK), lambda r: (r, 0, 0, 0)),
            pl.BlockSpec(memory_space=pltpu.VMEM),
        ],
        out_specs=pl.BlockSpec((ROWS_STEP, CPL, RANK, 128), lambda r: (r, 0, 0, 0)),
        out_shape=jax.ShapeDtypeStruct((ROW, CPL, RANK, 128), BF16),
        compiler_params=params(),
        cost_estimate=cost(17),
        name="couple_left",
    )(s, um)


def right_kernel(where_ref, z_ref, a_ref, b_ref, c_ref, d_ref, out_ref, win_ref, sems):
    @pl.when(pl.program_id(0) == 0)
    def _():
        copies = []
        begin = 0
        for k, piece in enumerate((a_ref, b_ref, c_ref, d_ref)):
            amount = piece.shape[0]
            target = win_ref.at[pl.ds(begin, amount)]
            copies.append(pltpu.make_async_copy(piece, target, sems.at[k]))
            begin += amount
        for copy in copies:
            copy.start()
        for copy in copies:
            copy.wait()

    first = pl.program_id(0) * ROWS_STEP
    down = lax.broadcasted_iota(jnp.int32, (RANK, RANK), 0)
    over = lax.broadcasted_iota(jnp.int32, (RANK, RANK), 1)

    def one(r, carry):
        for c in range(CPL):
            code = where_ref[first + r, c]
            unit = code // 64
            local = code % 64
            quarter = local // QUART
            x = win_ref[unit * UNIT + local % QUART]
            plain = jnp.where(quarter % 2 == 0, x[:, 0:RANK], x[:, RANK:128])
            turned = plain.T
            diag = win_ref[unit * UNIT + QUART, pl.ds(local, 1), 0:RANK]
            second = quarter >= 2
            strict = jnp.where(second, plain, turned)
            on = jnp.where(second, jnp.broadcast_to(diag, (RANK, RANK)), turned)
            lower = jnp.where(down > over, strict, jnp.where(down == over, on, 0.0))
            high, low = split(lower)
            z = z_ref[r, c]
            dot = functools.partial(
                lax.dot_general, dimension_numbers=NN, preferred_element_type=F32
            )
            out_ref[r, c] = dot(z, jnp.concatenate([high, high], axis=0)) + dot(z[:, 0:RANK], low)
        return carry

    lax.fori_loop(0, ROWS_STEP, one, 0, unroll=4)


def right_call(where, z, pieces):
    return pl.pallas_call(
        right_kernel,
        grid_spec=pltpu.PrefetchScalarGridSpec(
            num_scalar_prefetch=1,
            grid=(ROW // ROWS_STEP,),
            in_specs=[
                pl.BlockSpec((ROWS_STEP, CPL, RANK, 128), lambda r, w: (r, 0, 0, 0)),
            ]
            + [pl.BlockSpec(memory_space=pl.ANY)] * 4,
            out_specs=pl.BlockSpec((ROWS_STEP, CPL, RANK, RANK), lambda r, w: (r, 0, 0, 0)),
            scratch_shapes=[
                pltpu.VMEM((3 * COLUMN * UNIT, RANK, 128), F32),
                pltpu.SemaphoreType.DMA((4,)),
            ],
        ),
        out_shape=jax.ShapeDtypeStruct((ROW, CPL, RANK, RANK), F32),
        compiler_params=params(),
        cost_estimate=cost(20),
        name="couple_right",
    )(where, z, *pieces)


def shifted(array, axis, by):
    devices = lax.axis_size(axis)
    pairs = [(i, i + by) for i in range(devices) if 0 <= i + by < devices]
    return lax.ppermute(array, axis, pairs)


def swapped(array):
    devices = lax.axis_size("leaf")
    return lax.ppermute(array, "leaf", [(i, i ^ 1) for i in range(devices)])


def turned_column(array, by):
    devices = lax.axis_size("leaf")
    pairs = [(i, i // COLUMN * COLUMN + (i % COLUMN + 2 * by) % COLUMN) for i in range(devices)]
    return lax.ppermute(array, "leaf", pairs)


def together(*values):
    return lax.optimization_barrier(values)


def on_device(leaf_bases, transfers, top_transfers, couplings, coupling_cols):
    own = lax.axis_index("leaf").astype(jnp.int32)
    device_of = coupling_cols // ROW
    side = device_of // COLUMN - own // COLUMN
    steps = (own % COLUMN // 2 - device_of % COLUMN // 2) % (COLUMN // 2)
    other = (device_of + own) % 2
    place = jnp.where(
        side == 0, 4 * other + steps, 8 + 8 * other + 2 * steps + (side > 0).astype(jnp.int32)
    )
    where = place * 64 + coupling_cols % ROW

    grams, carried = gram_call(leaf_bases, transfers)
    frontier = lax.all_gather(carried, "leaf", axis=0, tiled=False)
    wide, unit = factor_call(grams)
    unit = unit.reshape(UNIT, RANK, 128)
    before = shifted(unit, "leaf", COLUMN)
    after = shifted(unit, "leaf", -COLUMN)
    line = [unit] + [turned_column(unit, by) for by in (1, 2, 3)]
    um = turn_call(wide).reshape(RANK, RANK, 128)
    new_leaves, moved = apply_call(um, leaf_bases, transfers)
    moved, um, before, after, *line = together(moved, um, before, after, *line)

    near = jnp.concatenate(line, axis=0)
    near_other = swapped(near)
    pair = jnp.concatenate([before, after], axis=0)
    sides = [pair] + [turned_column(pair, by) for by in (1, 2, 3)]
    left = left_call(couplings, um)
    left, near_other, frontier = together(left, near_other, frontier)

    top_wide = top_gram_call(frontier, top_transfers)
    top_wide, left, *sides = together(top_wide, left, *sides)
    far = jnp.concatenate(sides, axis=0)
    far_other = swapped(far)
    new_top, root_factor, mine = top_out_call(
        own.reshape(1), top_wide, top_transfers, moved[NODES - 1]
    )
    new_transfers = moved.at[NODES - 1].set(mine)
    new_couplings = right_call(where, left, (near, near_other, far, far_other))
    return (new_leaves, new_transfers, new_top, root_factor, new_couplings)


def solution(mesh):
    in_specs = (
        P("leaf", None, None),
        P("leaf", None, None),
        P(),
        P("leaf", None, None, None),
        P("leaf", None),
    )
    out_specs = (
        P("leaf", None, None),
        P("leaf", None, None),
        P(),
        P(),
        P("leaf", None, None, None),
    )
    return jax.shard_map(
        on_device, mesh=mesh, in_specs=in_specs, out_specs=out_specs, check_vma=False
    )
```

```python
import functools

import jax
import jax.numpy as jnp
from jax import lax
from jax.experimental import pallas as pl
from jax.experimental.pallas import tpu as pltpu
from jax.sharding import PartitionSpec as P

RANK = 64
LEAF = 32
NODES = 63
ROW = 56
CPL = 8
QUART = 14
UNIT = QUART + 1
COLUMN = 8
TOPN = 127
ROWS_STEP = 8
UNROLL = 4
CHUNKS = 4
MIB = 1024 * 1024
F32 = jnp.float32
BF16 = jnp.bfloat16
FULL = lax.Precision.HIGHEST

NN = (((1,), (0,)), ((), ()))
NT = (((1,), (1,)), ((), ()))
TN = (((0,), (0,)), ((), ()))


def exact(a, b, dims):
    return lax.dot_general(a, b, dims, precision=FULL, preferred_element_type=F32)


def split(a):
    high = a.astype(BF16)
    return high, (a - high.astype(F32)).astype(BF16)


def three(a, b, dims):
    ah, al = a
    bh, bl = b
    dot = functools.partial(lax.dot_general, dimension_numbers=dims, preferred_element_type=F32)
    return dot(ah, bh) + (dot(ah, bl) + dot(al, bh))


def mul3(a, b, dims):
    return three(split(a), split(b), dims)


def cost(us):
    return pl.CostEstimate(flops=us * 1_000_000, bytes_accessed=us * 2_500_000, transcendentals=0)


def params(mib):
    return pltpu.CompilerParams(vmem_limit_bytes=mib * MIB)


def load_lanes(g_ref, w_ref):
    place = lax.broadcasted_iota(jnp.int32, (RANK, 128), 0)

    def body(i, carry):
        block = g_ref[pl.ds(i, 128, stride=RANK), :].T
        w_ref[i, 0:RANK, :] = block[0:RANK]
        w_ref[i, RANK:128, :] = jnp.where(place == i, 1.0, 0.0).astype(F32)
        return carry

    lax.fori_loop(0, RANK, body, 0, unroll=8)


def eliminate(w_ref):
    for band in range(16):
        q = band // 2
        lo, hi = 8 * q, RANK + 8 * (q + 1)
        first = 4 * band
        rows = tuple(w_ref[first + a, lo:hi, :] for a in range(4))

        def step(k, rows):
            src = w_ref[k, lo:hi, :]
            return tuple(
                rows[a] - w_ref[k, first + a : first + a + 1, :] * src for a in range(4)
            )

        if first > 0:
            rows = lax.fori_loop(0, first, step, rows, unroll=4)
        rows = list(rows)
        for a in range(4):
            at = first + a - lo
            for b in range(a):
                rows[a] = rows[a] - rows[b][at : at + 1] * rows[b]
            pivot = rows[a][at : at + 1]
            scale = lax.rsqrt(pivot)
            scale = scale * (1.5 - 0.5 * pivot * scale * scale)
            rows[a] = rows[a] * scale
            w_ref[first + a, lo:hi, :] = rows[a]


def store_lanes(w_ref, um_ref, amount):
    place = lax.broadcasted_iota(jnp.int32, (RANK, 128), 0)

    def body(i, carry):
        upper = jnp.where(place >= i, w_ref[i, 0:RANK, :], 0.0)
        block = jnp.concatenate([upper, w_ref[i, RANK:128, :]], axis=0).T
        um_ref[pl.ds(i, amount, stride=RANK), :] = block[0:amount]
        return carry

    lax.fori_loop(0, RANK, body, 0, unroll=8)


def block_at(n):
    return pl.ds(pl.multiple_of(n * RANK, RANK), RANK)


def gram_kernel(v_hbm, e_hbm, g_ref, c_ref, v_ref, e_ref, sems):
    chunk = LEAF // CHUNKS
    copies = [
        pltpu.make_async_copy(
            v_hbm.at[pl.ds(k * chunk, chunk)], v_ref.at[pl.ds(k * chunk, chunk)], sems.at[k]
        )
        for k in range(CHUNKS)
    ]
    copies.append(pltpu.make_async_copy(e_hbm, e_ref, sems.at[CHUNKS]))
    for copy in copies:
        copy.start()

    def leaf(b, carry):
        v = v_ref[b]
        g_ref[block_at(b), 0:RANK] = exact(v, v, NT)
        return carry

    for k in range(CHUNKS):
        copies[k].wait()
        lax.fori_loop(k * chunk, (k + 1) * chunk, leaf, 0, unroll=chunk)
    copies[CHUNKS].wait()

    def parent(p, carry):
        a = 2 * (p - LEAF)
        ea, eb = e_ref[a], e_ref[a + 1]
        ga = g_ref[block_at(a), 0:RANK]
        gb = g_ref[block_at(a + 1), 0:RANK]
        both = jnp.concatenate([exact(ga, ea, NN), exact(gb, eb, NN)], axis=0)
        g_ref[block_at(p), 0:RANK] = exact(
            jnp.concatenate([ea, eb], axis=0), both, TN
        )
        return carry

    start, amount = LEAF, LEAF // 2
    while amount >= 1:
        lax.fori_loop(start, start + amount, parent, 0, unroll=min(amount, 16))
        start, amount = start + amount, amount // 2
    root = e_ref[NODES - 1]
    top = exact(root, exact(g_ref[(NODES - 1) * RANK : NODES * RANK, 0:RANK], root, NN), TN)
    c_ref[:, 0:RANK] = top[0:32]
    c_ref[:, RANK:128] = top[32:64]
    g_ref[NODES * RANK :, :] = jnp.zeros_like(g_ref[NODES * RANK :, :])


def gram_call(v, e):
    return pl.pallas_call(
        gram_kernel,
        out_shape=(
            jax.ShapeDtypeStruct((128 * RANK, 128), F32),
            jax.ShapeDtypeStruct((32, 128), F32),
        ),
        in_specs=[pl.BlockSpec(memory_space=pl.ANY)] * 2,
        scratch_shapes=[
            pltpu.VMEM(v.shape, F32),
            pltpu.VMEM(e.shape, F32),
            pltpu.SemaphoreType.DMA((CHUNKS + 1,)),
        ],
        compiler_params=params(62),
        cost_estimate=cost(12),
        name="gram_up",
    )(v, e)


def factor_kernel(g_ref, um_ref, unit_ref, w_ref):
    load_lanes(g_ref, w_ref)
    eliminate(w_ref)
    place = lax.broadcasted_iota(jnp.int32, (RANK, 128), 0)
    rows = w_ref.reshape(RANK * 128, 128)

    def pack(i, diag):
        upper = w_ref[i, 0:RANK, :]
        lower = rows[pl.ds(i, RANK, stride=128), :]
        other = pltpu.roll(lower, 128 - 2 * QUART, axis=1)
        mixed = jnp.where(place >= i, upper, other)
        both = jnp.concatenate([mixed, pltpu.roll(mixed, 128 - QUART, axis=1)], axis=0).T
        unit_ref[pl.ds(i, QUART, stride=RANK), :] = both[0:QUART]
        return jnp.where(place == i, lower, diag)

    diag = lax.fori_loop(0, RANK, pack, jnp.zeros((RANK, 128), F32), unroll=8)
    unit_ref[QUART * RANK :, :] = jnp.concatenate([diag, diag], axis=0).T[0:RANK]
    store_lanes(w_ref, um_ref, RANK)


def factor_call(g):
    return pl.pallas_call(
        factor_kernel,
        out_shape=(
            jax.ShapeDtypeStruct((RANK * RANK, 128), F32),
            jax.ShapeDtypeStruct((UNIT * RANK, 128), F32),
        ),
        scratch_shapes=[pltpu.VMEM((RANK, 128, 128), F32)],
        compiler_params=params(48),
        cost_estimate=cost(15),
        name="factor_local",
    )(g)


def apply_kernel(um_ref, v_ref, e_ref, top_ref, leaves_ref, moved_ref):
    def leaf(b, carry):
        m = um_ref[b, :, RANK:128]
        leaves_ref[b] = mul3(m, v_ref[b], NN)
        return carry

    lax.fori_loop(0, LEAF, leaf, 0, unroll=8)

    def parent(p, carry):
        a = 2 * (p - LEAF)
        pa = mul3(um_ref[a, :, 0:RANK], e_ref[a], NN)
        pb = mul3(um_ref[a + 1, :, 0:RANK], e_ref[a + 1], NN)
        q = mul3(jnp.concatenate([pa, pb], axis=0), um_ref[p, :, RANK:128], NT)
        moved_ref[a] = q[0:RANK]
        moved_ref[a + 1] = q[RANK:128]
        return carry

    lax.fori_loop(LEAF, NODES - 1, parent, 0, unroll=10)
    parent(NODES - 1, 0)
    moved_ref[NODES - 1] = mul3(um_ref[NODES - 1, :, 0:RANK], e_ref[NODES - 1], NN)


def apply_call(um, v, e, top):
    vm = pl.BlockSpec(memory_space=pltpu.VMEM)
    return pl.pallas_call(
        apply_kernel,
        in_specs=[vm, vm, vm, pl.BlockSpec(memory_space=pl.ANY)],
        out_shape=(
            jax.ShapeDtypeStruct(v.shape, F32),
            jax.ShapeDtypeStruct(e.shape, F32),
        ),
        compiler_params=params(48),
        cost_estimate=cost(9),
        name="apply_local",
    )(um, v, e, top)


def top_kernel(own_ref, c_ref, e_ref, p_ref, new_ref, root_ref, mine_ref, g_ref, w_ref, um_ref):
    def first(p, carry):
        x = c_ref[p]
        g_ref[block_at(63 + p), 0:RANK] = jnp.concatenate([x[:, 0:RANK], x[:, RANK:128]], axis=0)
        return carry

    lax.fori_loop(0, 64, first, 0, unroll=16)

    def join(n, carry):
        c = 2 * n + 1
        ea, eb = e_ref[c - 1], e_ref[c]
        ga = g_ref[block_at(c), 0:RANK]
        gb = g_ref[block_at(c + 1), 0:RANK]
        both = jnp.concatenate([exact(ga, ea, NN), exact(gb, eb, NN)], axis=0)
        g_ref[block_at(n), 0:RANK] = exact(jnp.concatenate([ea, eb], axis=0), both, TN)
        return carry

    for level in range(5, -1, -1):
        begin = 2**level - 1
        lax.fori_loop(begin, 2 * begin + 1, join, 0, unroll=min(2**level, 16))
    g_ref[TOPN * RANK :, :] = jnp.zeros_like(g_ref[TOPN * RANK :, :])
    load_lanes(g_ref, w_ref)
    eliminate(w_ref)
    store_lanes(w_ref, um_ref, 128)

    def out(n, carry):
        c = 2 * n + 1
        pa = mul3(um_ref[block_at(c), 0:RANK], e_ref[c - 1], NN)
        pb = mul3(um_ref[block_at(c + 1), 0:RANK], e_ref[c], NN)
        m = um_ref[block_at(n), RANK:128]
        q = mul3(jnp.concatenate([pa, pb], axis=0), m, NT)
        new_ref[c - 1] = q[0:RANK]
        new_ref[c] = q[RANK:128]
        return carry

    lax.fori_loop(0, 63, out, 0, unroll=9)
    root_ref[...] = um_ref[0:RANK, 0:RANK]
    up = um_ref[block_at(63 + own_ref[0] // 2), RANK:128]
    mine_ref[...] = mul3(p_ref[...], up, NT)


def top_call(own, c, e, p):
    vm = pl.BlockSpec(memory_space=pltpu.VMEM)
    return pl.pallas_call(
        top_kernel,
        in_specs=[pl.BlockSpec(memory_space=pltpu.SMEM), vm, vm, vm],
        out_shape=(
            jax.ShapeDtypeStruct(e.shape, F32),
            jax.ShapeDtypeStruct((RANK, RANK), F32),
            jax.ShapeDtypeStruct((RANK, RANK), F32),
        ),
        scratch_shapes=[
            pltpu.VMEM((128 * RANK, 128), F32),
            pltpu.VMEM((RANK, 128, 128), F32),
            pltpu.VMEM((128 * RANK, 128), F32),
        ],
        compiler_params=params(48),
        cost_estimate=cost(42),
        name="top_tree",
    )(own, c, e, p)


def couple_kernel(where_ref, s_ref, um_ref, *refs):
    *piece_refs, out_ref, win_ref, sems = refs

    @pl.when(pl.program_id(0) == 0)
    def _():
        copies = []
        begin = 0
        for k, piece in enumerate(piece_refs):
            amount = piece.shape[0]
            target = win_ref.at[pl.ds(begin, amount)]
            copies.append(pltpu.make_async_copy(piece, target, sems.at[k]))
            begin += amount
        for copy in copies:
            copy.start()
        for copy in copies:
            copy.wait()

    first = pl.program_id(0) * ROWS_STEP
    down = lax.broadcasted_iota(jnp.int32, (RANK, RANK), 0)
    over = lax.broadcasted_iota(jnp.int32, (RANK, RANK), 1)

    def one(r, carry):
        row = first + r
        rights = []
        for c in range(CPL):
            code = where_ref[row, c]
            unit = code // 64
            local = code % 64
            quarter = local // QUART
            x = win_ref[unit * UNIT + local % QUART]
            plain = jnp.where(quarter % 2 == 0, x[:, 0:RANK], x[:, RANK:128])
            turned = plain.T
            diag = win_ref[unit * UNIT + QUART, pl.ds(local, 1), 0:RANK]
            second = quarter >= 2
            strict = jnp.where(second, plain, turned)
            on = jnp.where(second, jnp.broadcast_to(diag, (RANK, RANK)), turned)
            lower = jnp.where(down > over, strict, jnp.where(down == over, on, 0.0))
            rights.append(mul3(s_ref[r, c], lower, NN))
        u = split(um_ref[row, :, 0:RANK])
        for c in range(CPL):
            out_ref[r, c] = three(u, split(rights[c]), NN)
        return carry

    lax.fori_loop(0, ROWS_STEP, one, 0, unroll=UNROLL)


def couple_call(where, s, um, pieces):
    def block():
        return pl.BlockSpec((ROWS_STEP, CPL, RANK, RANK), lambda r, w: (r, 0, 0, 0))

    return pl.pallas_call(
        couple_kernel,
        grid_spec=pltpu.PrefetchScalarGridSpec(
            num_scalar_prefetch=1,
            grid=(ROW // ROWS_STEP,),
            in_specs=[block(), pl.BlockSpec(memory_space=pltpu.VMEM)]
            + [pl.BlockSpec(memory_space=pl.ANY)] * len(pieces),
            out_specs=block(),
            scratch_shapes=[
                pltpu.VMEM((3 * COLUMN * UNIT, RANK, 128), F32),
                pltpu.SemaphoreType.DMA((len(pieces),)),
            ],
        ),
        out_shape=jax.ShapeDtypeStruct((ROW, CPL, RANK, RANK), F32),
        compiler_params=params(28),
        cost_estimate=cost(32),
        name="couple",
    )(where, s, um, *pieces)


def shifted(array, axis, by):
    devices = lax.axis_size(axis)
    pairs = [(i, i + by) for i in range(devices) if 0 <= i + by < devices]
    return lax.ppermute(array, axis, pairs)


def swapped(array):
    devices = lax.axis_size("leaf")
    return lax.ppermute(array, "leaf", [(i, i ^ 1) for i in range(devices)])


def turned_column(array, by):
    devices = lax.axis_size("leaf")
    pairs = [(i, i // COLUMN * COLUMN + (i % COLUMN + 2 * by) % COLUMN) for i in range(devices)]
    return lax.ppermute(array, "leaf", pairs)


def together(*values):
    return lax.optimization_barrier(values)


def on_device(leaf_bases, transfers, top_transfers, couplings, coupling_cols):
    own = lax.axis_index("leaf").astype(jnp.int32)
    device_of = coupling_cols // ROW
    side = device_of // COLUMN - own // COLUMN
    steps = (own % COLUMN // 2 - device_of % COLUMN // 2) % (COLUMN // 2)
    other = (device_of + own) % 2
    place = jnp.where(
        side == 0, steps, 4 + 2 * steps + (side > 0).astype(jnp.int32)
    ) + 12 * other
    where = place * 64 + coupling_cols % ROW

    devices = lax.axis_size("leaf")
    columns = devices // COLUMN
    along = [[c * COLUMN + j for j in range(COLUMN)] for c in range(columns)]
    across = [[c * COLUMN + j for c in range(columns)] for j in range(COLUMN)]
    grams, carried = gram_call(leaf_bases, transfers)
    joined = lax.all_gather(carried, "leaf", axis_index_groups=along, axis=0, tiled=False)
    joined = joined[0::2] + joined[1::2]
    joined, grams = together(joined, grams)
    frontier = lax.all_gather(joined, "leaf", axis_index_groups=across, axis=0, tiled=True)

    um, unit = factor_call(grams)
    um = um.reshape(RANK, RANK, 128)
    unit = unit.reshape(UNIT, RANK, 128)
    before = shifted(unit, "leaf", COLUMN)
    after = shifted(unit, "leaf", -COLUMN)
    line = [unit] + [turned_column(unit, by) for by in (1, 2, 3)]
    new_leaves, moved = apply_call(um, leaf_bases, transfers, top_transfers)
    pair = jnp.concatenate([before, after], axis=0)
    pair, moved, um, *line = together(pair, moved, um, *line)
    sides = [pair] + [turned_column(pair, by) for by in (1, 2, 3)]
    new_top, root_factor, mine = top_call(
        own.reshape(1), frontier, top_transfers, moved[NODES - 1]
    )
    mine, *rest = together(mine, *line, *sides)
    line, sides = rest[0:4], rest[4:8]
    line_other = [swapped(part) for part in line]
    sides_other = [swapped(part) for part in sides]
    new_transfers = moved.at[NODES - 1].set(mine)
    new_couplings = couple_call(where, couplings, um, line + sides + line_other + sides_other)
    return (new_leaves, new_transfers, new_top, root_factor, new_couplings)


def solution(mesh):
    in_specs = (
        P("leaf", None, None),
        P("leaf", None, None),
        P(),
        P("leaf", None, None, None),
        P("leaf", None),
    )
    out_specs = (
        P("leaf", None, None),
        P("leaf", None, None),
        P(),
        P(),
        P("leaf", None, None, None),
    )
    return jax.shard_map(
        on_device, mesh=mesh, in_specs=in_specs, out_specs=out_specs, check_vma=False
    )
```

```python
import functools

import jax
import jax.numpy as jnp
from jax import lax
from jax.experimental import pallas as pl
from jax.experimental.pallas import tpu as pltpu
from jax.sharding import PartitionSpec as P

RANK = 64
LEAF = 32
NODES = 63
ROW = 56
CPL = 8
QUART = 14
UNIT = QUART + 1
COLUMN = 8
TOPN = 127
ROWS_STEP = 8
UNROLL = 4
CHUNKS = 4
MIB = 1024 * 1024
F32 = jnp.float32
BF16 = jnp.bfloat16
FULL = lax.Precision.HIGHEST

NN = (((1,), (0,)), ((), ()))
NT = (((1,), (1,)), ((), ()))
TN = (((0,), (0,)), ((), ()))


def exact(a, b, dims):
    return lax.dot_general(a, b, dims, precision=FULL, preferred_element_type=F32)


def split(a):
    high = a.astype(BF16)
    return high, (a - high.astype(F32)).astype(BF16)


def three(a, b, dims):
    ah, al = a
    bh, bl = b
    dot = functools.partial(lax.dot_general, dimension_numbers=dims, preferred_element_type=F32)
    return dot(ah, bh) + (dot(ah, bl) + dot(al, bh))


def mul3(a, b, dims):
    return three(split(a), split(b), dims)


def cost(us):
    return pl.CostEstimate(flops=us * 1_000_000, bytes_accessed=us * 2_500_000, transcendentals=0)


def params(mib):
    return pltpu.CompilerParams(vmem_limit_bytes=mib * MIB)


def load_lanes(g_ref, w_ref, amount):
    place = lax.broadcasted_iota(jnp.int32, (RANK, 128), 0)

    def body(i, carry):
        block = g_ref[pl.ds(i, amount, stride=RANK), :].T
        w_ref[i, 0:RANK, 0:amount] = block[0:RANK]
        w_ref[i, RANK:128, :] = jnp.where(place == i, 1.0, 0.0).astype(F32)
        return carry

    lax.fori_loop(0, RANK, body, 0, unroll=8)


def eliminate(w_ref):
    for band in range(16):
        q = band // 2
        lo, hi = 8 * q, RANK + 8 * (q + 1)
        first = 4 * band
        rows = tuple(w_ref[first + a, lo:hi, :] for a in range(4))

        def step(k, rows):
            src = w_ref[k, lo:hi, :]
            return tuple(
                rows[a] - w_ref[k, first + a : first + a + 1, :] * src for a in range(4)
            )

        if first > 0:
            rows = lax.fori_loop(0, first, step, rows, unroll=4)
        rows = list(rows)
        for a in range(4):
            at = first + a - lo
            for b in range(a):
                rows[a] = rows[a] - rows[b][at : at + 1] * rows[b]
            pivot = rows[a][at : at + 1]
            scale = lax.rsqrt(pivot)
            scale = scale * (1.5 - 0.5 * pivot * scale * scale)
            rows[a] = rows[a] * scale
            w_ref[first + a, lo:hi, :] = rows[a]


def store_lanes(w_ref, um_ref, amount):
    place = lax.broadcasted_iota(jnp.int32, (RANK, 128), 0)

    def body(i, carry):
        upper = jnp.where(place >= i, w_ref[i, 0:RANK, :], 0.0)
        block = jnp.concatenate([upper, w_ref[i, RANK:128, :]], axis=0).T
        um_ref[pl.ds(i, amount, stride=RANK), :] = block[0:amount]
        return carry

    lax.fori_loop(0, RANK, body, 0, unroll=8)


def block_at(n):
    return pl.ds(pl.multiple_of(n * RANK, RANK), RANK)


def gram_kernel(v_hbm, e_hbm, g_ref, c_ref, v_ref, e_ref, sems):
    chunk = LEAF // CHUNKS
    copies = [
        pltpu.make_async_copy(
            v_hbm.at[pl.ds(k * chunk, chunk)], v_ref.at[pl.ds(k * chunk, chunk)], sems.at[k]
        )
        for k in range(CHUNKS)
    ]
    copies.append(pltpu.make_async_copy(e_hbm, e_ref, sems.at[CHUNKS]))
    for copy in copies:
        copy.start()

    def leaf(b, carry):
        v = v_ref[b]
        g_ref[block_at(b), 0:RANK] = exact(v, v, NT)
        return carry

    for k in range(CHUNKS):
        copies[k].wait()
        lax.fori_loop(k * chunk, (k + 1) * chunk, leaf, 0, unroll=chunk)
    copies[CHUNKS].wait()

    def parent(p, carry):
        a = 2 * (p - LEAF)
        ea, eb = e_ref[a], e_ref[a + 1]
        ga = g_ref[block_at(a), 0:RANK]
        gb = g_ref[block_at(a + 1), 0:RANK]
        both = jnp.concatenate([exact(ga, ea, NN), exact(gb, eb, NN)], axis=0)
        g_ref[block_at(p), 0:RANK] = exact(
            jnp.concatenate([ea, eb], axis=0), both, TN
        )
        return carry

    start, amount = LEAF, LEAF // 2
    while amount >= 1:
        lax.fori_loop(start, start + amount, parent, 0, unroll=min(amount, 16))
        start, amount = start + amount, amount // 2
    root = e_ref[NODES - 1]
    top = exact(root, exact(g_ref[(NODES - 1) * RANK : NODES * RANK, 0:RANK], root, NN), TN)
    c_ref[:, 0:RANK] = top[0:32]
    c_ref[:, RANK:128] = top[32:64]
    g_ref[NODES * RANK :, :] = jnp.zeros_like(g_ref[NODES * RANK :, :])


def gram_call(v, e):
    return pl.pallas_call(
        gram_kernel,
        out_shape=(
            jax.ShapeDtypeStruct((RANK * RANK, 128), F32),
            jax.ShapeDtypeStruct((32, 128), F32),
        ),
        in_specs=[pl.BlockSpec(memory_space=pl.ANY)] * 2,
        scratch_shapes=[
            pltpu.VMEM(v.shape, F32),
            pltpu.VMEM(e.shape, F32),
            pltpu.SemaphoreType.DMA((CHUNKS + 1,)),
        ],
        compiler_params=params(62),
        cost_estimate=cost(12),
        name="gram_up",
    )(v, e)


def factor_kernel(g_ref, um_ref, unit_ref, w_ref):
    load_lanes(g_ref, w_ref, RANK)
    eliminate(w_ref)
    place = lax.broadcasted_iota(jnp.int32, (RANK, 128), 0)
    rows = w_ref.reshape(RANK * 128, 128)

    def pack(i, diag):
        upper = w_ref[i, 0:RANK, :]
        lower = rows[pl.ds(i, RANK, stride=128), :]
        other = pltpu.roll(lower, 128 - 2 * QUART, axis=1)
        mixed = jnp.where(place >= i, upper, other)
        both = jnp.concatenate([mixed, pltpu.roll(mixed, 128 - QUART, axis=1)], axis=0).T
        unit_ref[pl.ds(i, QUART, stride=RANK), :] = both[0:QUART]
        return jnp.where(place == i, lower, diag)

    diag = lax.fori_loop(0, RANK, pack, jnp.zeros((RANK, 128), F32), unroll=8)
    unit_ref[QUART * RANK :, :] = jnp.concatenate([diag, diag], axis=0).T[0:RANK]
    store_lanes(w_ref, um_ref, RANK)


def factor_call(g):
    return pl.pallas_call(
        factor_kernel,
        out_shape=(
            jax.ShapeDtypeStruct((RANK * RANK, 128), F32),
            jax.ShapeDtypeStruct((UNIT * RANK, 128), F32),
        ),
        scratch_shapes=[pltpu.VMEM((RANK, 128, 128), F32)],
        compiler_params=params(48),
        cost_estimate=cost(15),
        name="factor_local",
    )(g)


def apply_kernel(um_ref, v_ref, e_ref, top_ref, leaves_ref, moved_ref):
    def leaf(b, carry):
        m = um_ref[b, :, RANK:128]
        leaves_ref[b] = mul3(m, v_ref[b], NN)
        return carry

    lax.fori_loop(0, LEAF, leaf, 0, unroll=8)

    def parent(p, carry):
        a = 2 * (p - LEAF)
        pa = mul3(um_ref[a, :, 0:RANK], e_ref[a], NN)
        pb = mul3(um_ref[a + 1, :, 0:RANK], e_ref[a + 1], NN)
        q = mul3(jnp.concatenate([pa, pb], axis=0), um_ref[p, :, RANK:128], NT)
        moved_ref[a] = q[0:RANK]
        moved_ref[a + 1] = q[RANK:128]
        return carry

    lax.fori_loop(LEAF, NODES - 1, parent, 0, unroll=10)
    parent(NODES - 1, 0)
    moved_ref[NODES - 1] = mul3(um_ref[NODES - 1, :, 0:RANK], e_ref[NODES - 1], NN)


def apply_call(um, v, e, top):
    vm = pl.BlockSpec(memory_space=pltpu.VMEM)
    return pl.pallas_call(
        apply_kernel,
        in_specs=[vm, vm, vm, pl.BlockSpec(memory_space=pl.ANY)],
        out_shape=(
            jax.ShapeDtypeStruct(v.shape, F32),
            jax.ShapeDtypeStruct(e.shape, F32),
        ),
        compiler_params=params(48),
        cost_estimate=cost(9),
        name="apply_local",
    )(um, v, e, top)


def top_kernel(own_ref, c_ref, e_ref, p_ref, new_ref, root_ref, mine_ref, g_ref, w_ref, um_ref):
    def first(p, carry):
        x = c_ref[p]
        g_ref[block_at(63 + p), 0:RANK] = jnp.concatenate([x[:, 0:RANK], x[:, RANK:128]], axis=0)
        return carry

    lax.fori_loop(0, 64, first, 0, unroll=16)

    def join(n, carry):
        c = 2 * n + 1
        ea, eb = e_ref[c - 1], e_ref[c]
        ga = g_ref[block_at(c), 0:RANK]
        gb = g_ref[block_at(c + 1), 0:RANK]
        both = jnp.concatenate([exact(ga, ea, NN), exact(gb, eb, NN)], axis=0)
        g_ref[block_at(n), 0:RANK] = exact(jnp.concatenate([ea, eb], axis=0), both, TN)
        return carry

    for level in range(5, -1, -1):
        begin = 2**level - 1
        lax.fori_loop(begin, 2 * begin + 1, join, 0, unroll=min(2**level, 16))
    g_ref[TOPN * RANK :, :] = jnp.zeros_like(g_ref[TOPN * RANK :, :])
    load_lanes(g_ref, w_ref, 128)
    eliminate(w_ref)
    store_lanes(w_ref, um_ref, 128)

    def out(n, carry):
        c = 2 * n + 1
        pa = mul3(um_ref[block_at(c), 0:RANK], e_ref[c - 1], NN)
        pb = mul3(um_ref[block_at(c + 1), 0:RANK], e_ref[c], NN)
        m = um_ref[block_at(n), RANK:128]
        q = mul3(jnp.concatenate([pa, pb], axis=0), m, NT)
        new_ref[c - 1] = q[0:RANK]
        new_ref[c] = q[RANK:128]
        return carry

    lax.fori_loop(0, 63, out, 0, unroll=9)
    root_ref[...] = um_ref[0:RANK, 0:RANK]
    up = um_ref[block_at(63 + own_ref[0] // 2), RANK:128]
    mine_ref[...] = mul3(p_ref[...], up, NT)


def top_call(own, c, e, p):
    vm = pl.BlockSpec(memory_space=pltpu.VMEM)
    return pl.pallas_call(
        top_kernel,
        in_specs=[pl.BlockSpec(memory_space=pltpu.SMEM), vm, vm, vm],
        out_shape=(
            jax.ShapeDtypeStruct(e.shape, F32),
            jax.ShapeDtypeStruct((RANK, RANK), F32),
            jax.ShapeDtypeStruct((RANK, RANK), F32),
        ),
        scratch_shapes=[
            pltpu.VMEM((128 * RANK, 128), F32),
            pltpu.VMEM((RANK, 128, 128), F32),
            pltpu.VMEM((128 * RANK, 128), F32),
        ],
        compiler_params=params(62),
        cost_estimate=cost(42),
        name="top_tree",
    )(own, c, e, p)


def couple_kernel(where_ref, s_ref, um_ref, *refs):
    *piece_refs, out_ref, win_ref, sems = refs

    @pl.when(pl.program_id(0) == 0)
    def _():
        copies = []
        begin = 0
        for k, piece in enumerate(piece_refs):
            amount = piece.shape[0]
            target = win_ref.at[pl.ds(begin, amount)]
            copies.append(pltpu.make_async_copy(piece, target, sems.at[k]))
            begin += amount
        for copy in copies:
            copy.start()
        for copy in copies:
            copy.wait()

    first = pl.program_id(0) * ROWS_STEP
    down = lax.broadcasted_iota(jnp.int32, (RANK, RANK), 0)
    over = lax.broadcasted_iota(jnp.int32, (RANK, RANK), 1)

    def one(r, carry):
        row = first + r
        rights = []
        for c in range(CPL):
            code = where_ref[row, c]
            unit = code // 64
            local = code % 64
            quarter = local // QUART
            x = win_ref[unit * UNIT + local % QUART]
            plain = jnp.where(quarter % 2 == 0, x[:, 0:RANK], x[:, RANK:128])
            turned = plain.T
            diag = win_ref[unit * UNIT + QUART, pl.ds(local, 1), 0:RANK]
            second = quarter >= 2
            strict = jnp.where(second, plain, turned)
            on = jnp.where(second, jnp.broadcast_to(diag, (RANK, RANK)), turned)
            lower = jnp.where(down > over, strict, jnp.where(down == over, on, 0.0))
            rights.append(mul3(s_ref[r, c], lower, NN))
        u = split(um_ref[row, :, 0:RANK])
        for c in range(CPL):
            out_ref[r, c] = three(u, split(rights[c]), NN)
        return carry

    lax.fori_loop(0, ROWS_STEP, one, 0, unroll=UNROLL)


def couple_call(where, s, um, pieces):
    def block():
        return pl.BlockSpec((ROWS_STEP, CPL, RANK, RANK), lambda r, w: (r, 0, 0, 0))

    return pl.pallas_call(
        couple_kernel,
        grid_spec=pltpu.PrefetchScalarGridSpec(
            num_scalar_prefetch=1,
            grid=(ROW // ROWS_STEP,),
            in_specs=[block(), pl.BlockSpec(memory_space=pltpu.VMEM)]
            + [pl.BlockSpec(memory_space=pl.ANY)] * len(pieces),
            out_specs=block(),
            scratch_shapes=[
                pltpu.VMEM((3 * COLUMN * UNIT, RANK, 128), F32),
                pltpu.SemaphoreType.DMA((len(pieces),)),
            ],
        ),
        out_shape=jax.ShapeDtypeStruct((ROW, CPL, RANK, RANK), F32),
        compiler_params=params(62),
        cost_estimate=cost(32),
        name="couple",
    )(where, s, um, *pieces)


def shifted(array, axis, by):
    devices = lax.axis_size(axis)
    pairs = [(i, i + by) for i in range(devices) if 0 <= i + by < devices]
    return lax.ppermute(array, axis, pairs)


def swapped(array):
    devices = lax.axis_size("leaf")
    return lax.ppermute(array, "leaf", [(i, i ^ 1) for i in range(devices)])


def turned_column(array, by):
    devices = lax.axis_size("leaf")
    pairs = [(i, i // COLUMN * COLUMN + (i % COLUMN + 2 * by) % COLUMN) for i in range(devices)]
    return lax.ppermute(array, "leaf", pairs)


def together(*values):
    return lax.optimization_barrier(values)


def on_device(leaf_bases, transfers, top_transfers, couplings, coupling_cols):
    own = lax.axis_index("leaf").astype(jnp.int32)
    device_of = coupling_cols // ROW
    side = device_of // COLUMN - own // COLUMN
    steps = (own % COLUMN // 2 - device_of % COLUMN // 2) % (COLUMN // 2)
    other = (device_of + own) % 2
    place = jnp.where(
        side == 0, steps, 4 + 2 * steps + (side > 0).astype(jnp.int32)
    ) + 12 * other
    where = place * 64 + coupling_cols % ROW

    devices = lax.axis_size("leaf")
    columns = devices // COLUMN
    along = [[c * COLUMN + j for j in range(COLUMN)] for c in range(columns)]
    across = [[c * COLUMN + j for c in range(columns)] for j in range(COLUMN)]
    grams, carried = gram_call(leaf_bases, transfers)
    joined = lax.all_gather(carried, "leaf", axis_index_groups=along, axis=0, tiled=False)
    joined = joined[0::2] + joined[1::2]
    joined, grams = together(joined, grams)
    frontier = lax.all_gather(joined, "leaf", axis_index_groups=across, axis=0, tiled=True)

    um, unit = factor_call(grams)
    um = um.reshape(RANK, RANK, 128)
    unit = unit.reshape(UNIT, RANK, 128)
    before = shifted(unit, "leaf", COLUMN)
    after = shifted(unit, "leaf", -COLUMN)
    line = [unit] + [turned_column(unit, by) for by in (1, 2, 3)]
    new_leaves, moved = apply_call(um, leaf_bases, transfers, top_transfers)
    pair = jnp.concatenate([before, after], axis=0)
    pair, moved, um, *line = together(pair, moved, um, *line)
    line_other = [swapped(part) for part in line]
    sides = [pair] + [turned_column(pair, by) for by in (1, 2, 3)]
    new_top, root_factor, mine = top_call(
        own.reshape(1), frontier, top_transfers, moved[NODES - 1]
    )
    mine, *rest = together(mine, *line_other, *sides)
    line_other, sides = rest[0:4], rest[4:8]
    sides_other = [swapped(part) for part in sides]
    new_transfers = moved.at[NODES - 1].set(mine)
    new_couplings = couple_call(where, couplings, um, line + sides + line_other + sides_other)
    return (new_leaves, new_transfers, new_top, root_factor, new_couplings)


def solution(mesh):
    in_specs = (
        P("leaf", None, None),
        P("leaf", None, None),
        P(),
        P("leaf", None, None, None),
        P("leaf", None),
    )
    out_specs = (
        P("leaf", None, None),
        P("leaf", None, None),
        P(),
        P(),
        P("leaf", None, None, None),
    )
    return jax.shard_map(
        on_device, mesh=mesh, in_specs=in_specs, out_specs=out_specs, check_vma=False
    )
```

```python
import functools

import jax
import jax.numpy as jnp
from jax import lax
from jax.experimental import pallas as pl
from jax.experimental.pallas import tpu as pltpu
from jax.sharding import PartitionSpec as P

RANK = 64
LEAF = 32
NODES = 63
ROW = 56
CPL = 8
QUART = 14
UNIT = QUART + 1
COLUMN = 8
TOPN = 127
ROWS_STEP = 8
UNROLL = 8
CHUNKS = 4
MIB = 1024 * 1024
F32 = jnp.float32
BF16 = jnp.bfloat16
FULL = lax.Precision.HIGHEST

NN = (((1,), (0,)), ((), ()))
NT = (((1,), (1,)), ((), ()))
TN = (((0,), (0,)), ((), ()))


def exact(a, b, dims):
    return lax.dot_general(a, b, dims, precision=FULL, preferred_element_type=F32)


def split(a):
    high = a.astype(BF16)
    return high, (a - high.astype(F32)).astype(BF16)


def three(a, b, dims):
    ah, al = a
    bh, bl = b
    dot = functools.partial(lax.dot_general, dimension_numbers=dims, preferred_element_type=F32)
    return dot(ah, bh) + (dot(ah, bl) + dot(al, bh))


def mul3(a, b, dims):
    return three(split(a), split(b), dims)


def cost(us):
    return pl.CostEstimate(flops=us * 1_000_000, bytes_accessed=us * 2_500_000, transcendentals=0)


def params(mib):
    return pltpu.CompilerParams(vmem_limit_bytes=mib * MIB)


def load_lanes(g_ref, w_ref, amount):
    place = lax.broadcasted_iota(jnp.int32, (RANK, 128), 0)

    def body(i, carry):
        block = g_ref[pl.ds(i, amount, stride=RANK), :].T
        w_ref[i, 0:RANK, 0:amount] = block[0:RANK]
        w_ref[i, RANK:128, :] = jnp.where(place == i, 1.0, 0.0).astype(F32)
        return carry

    lax.fori_loop(0, RANK, body, 0, unroll=8)


def eliminate(w_ref):
    for band in range(16):
        q = band // 2
        lo, hi = 8 * q, RANK + 8 * (q + 1)
        first = 4 * band
        rows = tuple(w_ref[first + a, lo:hi, :] for a in range(4))

        def step(k, rows):
            src = w_ref[k, lo:hi, :]
            return tuple(
                rows[a] - w_ref[k, first + a : first + a + 1, :] * src for a in range(4)
            )

        if first > 0:
            rows = lax.fori_loop(0, first, step, rows, unroll=4)
        rows = list(rows)
        for a in range(4):
            at = first + a - lo
            for b in range(a):
                rows[a] = rows[a] - rows[b][at : at + 1] * rows[b]
            pivot = rows[a][at : at + 1]
            scale = lax.rsqrt(pivot)
            scale = scale * (1.5 - 0.5 * pivot * scale * scale)
            rows[a] = rows[a] * scale
            w_ref[first + a, lo:hi, :] = rows[a]


def store_lanes(w_ref, um_ref, amount):
    place = lax.broadcasted_iota(jnp.int32, (RANK, 128), 0)

    def body(i, carry):
        upper = jnp.where(place >= i, w_ref[i, 0:RANK, :], 0.0)
        block = jnp.concatenate([upper, w_ref[i, RANK:128, :]], axis=0).T
        um_ref[pl.ds(i, amount, stride=RANK), :] = block[0:amount]
        return carry

    lax.fori_loop(0, RANK, body, 0, unroll=8)


def block_at(n):
    return pl.ds(pl.multiple_of(n * RANK, RANK), RANK)


def gram_kernel(v_hbm, e_hbm, g_ref, c_ref, v_ref, e_ref, sems):
    chunk = LEAF // CHUNKS
    copies = [
        pltpu.make_async_copy(
            v_hbm.at[pl.ds(k * chunk, chunk)], v_ref.at[pl.ds(k * chunk, chunk)], sems.at[k]
        )
        for k in range(CHUNKS)
    ]
    copies.append(pltpu.make_async_copy(e_hbm, e_ref, sems.at[CHUNKS]))
    for copy in copies:
        copy.start()

    def leaf(b, carry):
        v = v_ref[b]
        g_ref[block_at(b), 0:RANK] = exact(v, v, NT)
        return carry

    for k in range(CHUNKS):
        copies[k].wait()
        lax.fori_loop(k * chunk, (k + 1) * chunk, leaf, 0, unroll=chunk)
    copies[CHUNKS].wait()

    def parent(p, carry):
        a = 2 * (p - LEAF)
        ea, eb = e_ref[a], e_ref[a + 1]
        ga = g_ref[block_at(a), 0:RANK]
        gb = g_ref[block_at(a + 1), 0:RANK]
        both = jnp.concatenate([exact(ga, ea, NN), exact(gb, eb, NN)], axis=0)
        g_ref[block_at(p), 0:RANK] = exact(
            jnp.concatenate([ea, eb], axis=0), both, TN
        )
        return carry

    start, amount = LEAF, LEAF // 2
    while amount >= 1:
        lax.fori_loop(start, start + amount, parent, 0, unroll=min(amount, 16))
        start, amount = start + amount, amount // 2
    root = e_ref[NODES - 1]
    top = exact(root, exact(g_ref[(NODES - 1) * RANK : NODES * RANK, 0:RANK], root, NN), TN)
    c_ref[:, 0:RANK] = top[0:32]
    c_ref[:, RANK:128] = top[32:64]
    g_ref[NODES * RANK :, :] = jnp.zeros_like(g_ref[NODES * RANK :, :])


def gram_call(v, e):
    return pl.pallas_call(
        gram_kernel,
        out_shape=(
            jax.ShapeDtypeStruct((RANK * RANK, 128), F32),
            jax.ShapeDtypeStruct((32, 128), F32),
        ),
        in_specs=[pl.BlockSpec(memory_space=pl.ANY)] * 2,
        scratch_shapes=[
            pltpu.VMEM(v.shape, F32),
            pltpu.VMEM(e.shape, F32),
            pltpu.SemaphoreType.DMA((CHUNKS + 1,)),
        ],
        compiler_params=params(62),
        cost_estimate=cost(12),
        name="gram_up",
    )(v, e)


def factor_kernel(g_ref, um_ref, unit_ref, w_ref):
    load_lanes(g_ref, w_ref, RANK)
    eliminate(w_ref)
    place = lax.broadcasted_iota(jnp.int32, (RANK, 128), 0)
    rows = w_ref.reshape(RANK * 128, 128)

    def pack(i, diag):
        upper = w_ref[i, 0:RANK, :]
        lower = rows[pl.ds(i, RANK, stride=128), :]
        other = pltpu.roll(lower, 128 - 2 * QUART, axis=1)
        mixed = jnp.where(place >= i, upper, other)
        both = jnp.concatenate([mixed, pltpu.roll(mixed, 128 - QUART, axis=1)], axis=0).T
        unit_ref[pl.ds(i, QUART, stride=RANK), :] = both[0:QUART]
        return jnp.where(place == i, lower, diag)

    diag = lax.fori_loop(0, RANK, pack, jnp.zeros((RANK, 128), F32), unroll=8)
    unit_ref[QUART * RANK :, :] = jnp.concatenate([diag, diag], axis=0).T[0:RANK]
    store_lanes(w_ref, um_ref, RANK)


def factor_call(g):
    return pl.pallas_call(
        factor_kernel,
        out_shape=(
            jax.ShapeDtypeStruct((RANK * RANK, 128), F32),
            jax.ShapeDtypeStruct((UNIT * RANK, 128), F32),
        ),
        scratch_shapes=[pltpu.VMEM((RANK, 128, 128), F32)],
        compiler_params=params(48),
        cost_estimate=cost(15),
        name="factor_local",
    )(g)


def apply_kernel(um_ref, v_ref, e_ref, top_ref, leaves_ref, moved_ref):
    def leaf(b, carry):
        m = um_ref[b, :, RANK:128]
        leaves_ref[b] = mul3(m, v_ref[b], NN)
        return carry

    lax.fori_loop(0, LEAF, leaf, 0, unroll=8)

    def parent(p, carry):
        a = 2 * (p - LEAF)
        pa = mul3(um_ref[a, :, 0:RANK], e_ref[a], NN)
        pb = mul3(um_ref[a + 1, :, 0:RANK], e_ref[a + 1], NN)
        q = mul3(jnp.concatenate([pa, pb], axis=0), um_ref[p, :, RANK:128], NT)
        moved_ref[a] = q[0:RANK]
        moved_ref[a + 1] = q[RANK:128]
        return carry

    lax.fori_loop(LEAF, NODES - 1, parent, 0, unroll=10)
    parent(NODES - 1, 0)
    moved_ref[NODES - 1] = mul3(um_ref[NODES - 1, :, 0:RANK], e_ref[NODES - 1], NN)


def apply_call(um, v, e, top):
    vm = pl.BlockSpec(memory_space=pltpu.VMEM)
    return pl.pallas_call(
        apply_kernel,
        in_specs=[vm, vm, vm, pl.BlockSpec(memory_space=pl.ANY)],
        out_shape=(
            jax.ShapeDtypeStruct(v.shape, F32),
            jax.ShapeDtypeStruct(e.shape, F32),
        ),
        compiler_params=params(48),
        cost_estimate=cost(9),
        name="apply_local",
    )(um, v, e, top)


def top_kernel(own_ref, c_ref, e_ref, p_ref, new_ref, root_ref, mine_ref, g_ref, w_ref, um_ref):
    def first(p, carry):
        x = c_ref[p]
        g_ref[block_at(63 + p), 0:RANK] = jnp.concatenate([x[:, 0:RANK], x[:, RANK:128]], axis=0)
        return carry

    lax.fori_loop(0, 64, first, 0, unroll=16)

    def join(n, carry):
        c = 2 * n + 1
        ea, eb = e_ref[c - 1], e_ref[c]
        ga = g_ref[block_at(c), 0:RANK]
        gb = g_ref[block_at(c + 1), 0:RANK]
        both = jnp.concatenate([exact(ga, ea, NN), exact(gb, eb, NN)], axis=0)
        g_ref[block_at(n), 0:RANK] = exact(jnp.concatenate([ea, eb], axis=0), both, TN)
        return carry

    for level in range(5, -1, -1):
        begin = 2**level - 1
        lax.fori_loop(begin, 2 * begin + 1, join, 0, unroll=2**level)
    g_ref[TOPN * RANK :, :] = jnp.zeros_like(g_ref[TOPN * RANK :, :])
    load_lanes(g_ref, w_ref, 128)
    eliminate(w_ref)
    store_lanes(w_ref, um_ref, 128)

    def out(n, carry):
        c = 2 * n + 1
        pa = mul3(um_ref[block_at(c), 0:RANK], e_ref[c - 1], NN)
        pb = mul3(um_ref[block_at(c + 1), 0:RANK], e_ref[c], NN)
        m = um_ref[block_at(n), RANK:128]
        q = mul3(jnp.concatenate([pa, pb], axis=0), m, NT)
        new_ref[c - 1] = q[0:RANK]
        new_ref[c] = q[RANK:128]
        return carry

    lax.fori_loop(0, 63, out, 0, unroll=21)
    root_ref[...] = um_ref[0:RANK, 0:RANK]
    up = um_ref[block_at(63 + own_ref[0] // 2), RANK:128]
    mine_ref[...] = mul3(p_ref[...], up, NT)


def top_call(own, c, e, p):
    vm = pl.BlockSpec(memory_space=pltpu.VMEM)
    return pl.pallas_call(
        top_kernel,
        in_specs=[pl.BlockSpec(memory_space=pltpu.SMEM), vm, vm, vm],
        out_shape=(
            jax.ShapeDtypeStruct(e.shape, F32),
            jax.ShapeDtypeStruct((RANK, RANK), F32),
            jax.ShapeDtypeStruct((RANK, RANK), F32),
        ),
        scratch_shapes=[
            pltpu.VMEM((128 * RANK, 128), F32),
            pltpu.VMEM((RANK, 128, 128), F32),
            pltpu.VMEM((128 * RANK, 128), F32),
        ],
        compiler_params=params(62),
        cost_estimate=cost(42),
        name="top_tree",
    )(own, c, e, p)


def couple_kernel(where_ref, s_ref, um_ref, *refs):
    *piece_refs, out_ref, win_ref, sems = refs

    @pl.when(pl.program_id(0) == 0)
    def _():
        copies = []
        begin = 0
        for k, piece in enumerate(piece_refs):
            amount = piece.shape[0]
            target = win_ref.at[pl.ds(begin, amount)]
            copies.append(pltpu.make_async_copy(piece, target, sems.at[k]))
            begin += amount
        for copy in copies:
            copy.start()
        for copy in copies:
            copy.wait()

    first = pl.program_id(0) * ROWS_STEP
    down = lax.broadcasted_iota(jnp.int32, (RANK, RANK), 0)
    over = lax.broadcasted_iota(jnp.int32, (RANK, RANK), 1)

    def one(r, carry):
        row = first + r
        rights = []
        for c in range(CPL):
            code = where_ref[row, c]
            unit = code // 64
            local = code % 64
            quarter = local // QUART
            x = win_ref[unit * UNIT + local % QUART]
            plain = jnp.where(quarter % 2 == 0, x[:, 0:RANK], x[:, RANK:128])
            turned = plain.T
            diag = win_ref[unit * UNIT + QUART, pl.ds(local, 1), 0:RANK]
            second = quarter >= 2
            strict = jnp.where(second, plain, turned)
            on = jnp.where(second, jnp.broadcast_to(diag, (RANK, RANK)), turned)
            lower = jnp.where(down > over, strict, jnp.where(down == over, on, 0.0))
            rights.append(mul3(s_ref[r, c], lower, NN))
        u = split(um_ref[row, :, 0:RANK])
        for c in range(CPL):
            out_ref[r, c] = three(u, split(rights[c]), NN)
        return carry

    lax.fori_loop(0, ROWS_STEP, one, 0, unroll=UNROLL)


def couple_call(where, s, um, pieces):
    def block():
        return pl.BlockSpec((ROWS_STEP, CPL, RANK, RANK), lambda r, w: (r, 0, 0, 0))

    return pl.pallas_call(
        couple_kernel,
        grid_spec=pltpu.PrefetchScalarGridSpec(
            num_scalar_prefetch=1,
            grid=(ROW // ROWS_STEP,),
            in_specs=[block(), pl.BlockSpec(memory_space=pltpu.VMEM)]
            + [pl.BlockSpec(memory_space=pl.ANY)] * len(pieces),
            out_specs=block(),
            scratch_shapes=[
                pltpu.VMEM((3 * COLUMN * UNIT, RANK, 128), F32),
                pltpu.SemaphoreType.DMA((len(pieces),)),
            ],
        ),
        out_shape=jax.ShapeDtypeStruct((ROW, CPL, RANK, RANK), F32),
        compiler_params=params(62),
        cost_estimate=cost(32),
        name="couple",
    )(where, s, um, *pieces)


def shifted(array, axis, by):
    devices = lax.axis_size(axis)
    pairs = [(i, i + by) for i in range(devices) if 0 <= i + by < devices]
    return lax.ppermute(array, axis, pairs)


def swapped(array):
    devices = lax.axis_size("leaf")
    return lax.ppermute(array, "leaf", [(i, i ^ 1) for i in range(devices)])


def turned_column(array, by):
    devices = lax.axis_size("leaf")
    pairs = [(i, i // COLUMN * COLUMN + (i % COLUMN + 2 * by) % COLUMN) for i in range(devices)]
    return lax.ppermute(array, "leaf", pairs)


def together(*values):
    return lax.optimization_barrier(values)


def on_device(leaf_bases, transfers, top_transfers, couplings, coupling_cols):
    own = lax.axis_index("leaf").astype(jnp.int32)
    device_of = coupling_cols // ROW
    side = device_of // COLUMN - own // COLUMN
    steps = (own % COLUMN // 2 - device_of % COLUMN // 2) % (COLUMN // 2)
    other = (device_of + own) % 2
    place = jnp.where(
        side == 0, steps, 4 + 2 * steps + (side > 0).astype(jnp.int32)
    ) + 12 * other
    where = place * 64 + coupling_cols % ROW

    devices = lax.axis_size("leaf")
    columns = devices // COLUMN
    along = [[c * COLUMN + j for j in range(COLUMN)] for c in range(columns)]
    across = [[c * COLUMN + j for c in range(columns)] for j in range(COLUMN)]
    grams, carried = gram_call(leaf_bases, transfers)
    joined = lax.all_gather(carried, "leaf", axis_index_groups=along, axis=0, tiled=False)
    joined = joined[0::2] + joined[1::2]
    joined, grams = together(joined, grams)
    frontier = lax.all_gather(joined, "leaf", axis_index_groups=across, axis=0, tiled=True)

    um, unit = factor_call(grams)
    um = um.reshape(RANK, RANK, 128)
    unit = unit.reshape(UNIT, RANK, 128)
    before = shifted(unit, "leaf", COLUMN)
    after = shifted(unit, "leaf", -COLUMN)
    line = [unit] + [turned_column(unit, by) for by in (1, 2, 3)]
    new_leaves, moved = apply_call(um, leaf_bases, transfers, top_transfers)
    pair = jnp.concatenate([before, after], axis=0)
    pair, moved, um, *line = together(pair, moved, um, *line)
    line_other = [swapped(part) for part in line]
    sides = [pair] + [turned_column(pair, by) for by in (1, 2, 3)]
    new_top, root_factor, mine = top_call(
        own.reshape(1), frontier, top_transfers, moved[NODES - 1]
    )
    mine, *rest = together(mine, *line_other, *sides)
    line_other, sides = rest[0:4], rest[4:8]
    sides_other = [swapped(part) for part in sides]
    new_transfers = moved.at[NODES - 1].set(mine)
    new_couplings = couple_call(where, couplings, um, line + sides + line_other + sides_other)
    return (new_leaves, new_transfers, new_top, root_factor, new_couplings)


def solution(mesh):
    in_specs = (
        P("leaf", None, None),
        P("leaf", None, None),
        P(),
        P("leaf", None, None, None),
        P("leaf", None),
    )
    out_specs = (
        P("leaf", None, None),
        P("leaf", None, None),
        P(),
        P(),
        P("leaf", None, None, None),
    )
    return jax.shard_map(
        on_device, mesh=mesh, in_specs=in_specs, out_specs=out_specs, check_vma=False
    )
```
